128 devices in a mesh: blk: 64 (over x_lo, y, z, core), rep: 2 (over x_hi).
Axes of the slice: x: 4 (x_hi: 2, x_lo: 2; x = x_hi * 2 + x_lo), y: 4, z: 4, core: 2. Of those that a mesh axis runs over, the one named last changes fastest.
Arguments:
- user_factors: float32 [65536, 256], P('blk'), may hold values from -4 to 4
- item_factors: float32 [32768, 256], P(('blk', 'rep')), may hold values from -4 to 4
- user_accum: float32 [65536, 256], P('blk'), may hold values from 0.05 to 0.5
- item_accum: float32 [32768, 256], P(('blk', 'rep')), may hold values from 0.05 to 0.5
- ratings: bfloat16 [64, 512, 128, 128], P('blk', 'rep'), may hold values from -16 to 16
- masks: bfloat16 [64, 512, 128, 128], P('blk', 'rep'), may hold values from -1 to 1
- tile_users: int32 [64, 512], P('blk', 'rep'), may hold values from 0 to 7
- tile_items: int32 [64, 512], P('blk', 'rep'), may hold values from 0 to 255, as said below
- tile_counts: int32 [64, 128], P('blk', 'rep'), may hold values from 1 to 4, as said below
Outputs:
- new_users: float32 [65536, 256], P('blk')
- new_items: float32 [32768, 256], P(('blk', 'rep'))
The draws below stay inside these ranges and needn't reach their ends.
Inputs may be any that keep to these rules, and one draw needn't show every extreme that they name: Slots q with q // 4 = g name item blocks of owner (g % 64) * 2 + g // 64 of the 2-block owners, i.e. tile_items[s, q] // 2 equals that owner; the first slot of each group names the owner's last block. `tile_counts`: each slab has some group with all 4 slots live.
All inputs are finite; a program needn't handle non-finite values.
Results may differ from the reference program's by a relative error of at most 0.0053.
Values may be sent and summed in bfloat16 or wider, within the bound.
No kernel may reach another device: no remote copies, remote signals or barrier semaphores. Data moves between devices by JAX's collectives and lax.ppermute only.
A program may use at most 128 MiB of HBM per device.

```python
import math
import jax
import jax.numpy as jnp
from jax import lax

R = 256
TILE = 128
USR_DEV = 1024
SLOTS = 4
IBD = 2
SLABS = 64
HALVES = 2
USERS = 65536
ITEMS = 32768
GROUPS = 512


def draw_tile_items(key, part):
    key = jax.random.fold_in(key, 23)
    column = jnp.arange(GROUPS, dtype=jnp.int32)
    half_index = column // (SLABS * SLOTS)
    owner_slab = column // SLOTS % SLABS
    first_slot = column % SLOTS == 0
    within = jax.random.randint(key, (SLABS, GROUPS), 0, IBD, dtype=jnp.int32)
    within = jnp.where(first_slot[None, :], IBD - 1, within)
    return ((owner_slab * HALVES + half_index) * IBD)[None, :] + within


def draw_tile_counts(key, part):
    key = jax.random.fold_in(key, 37)
    key_count, key_full = jax.random.split(key)
    counts = jax.random.randint(key_count, (SLABS, HALVES * SLABS), 1, SLOTS + 1, dtype=jnp.int32)
    full_at = jax.random.randint(key_full, (SLABS, 1), 0, HALVES * SLABS, dtype=jnp.int32)
    column = jnp.arange(HALVES * SLABS, dtype=jnp.int32)[None, :]
    return jnp.where(column == full_at, SLOTS, counts)


def touch_ends(drawn, stream_key, least, largest):
    place = [jax.random.randint(jax.random.fold_in(stream_key, axis), (), 0, length) for axis, length in enumerate(drawn.shape)]
    longest = drawn.shape.index(max(drawn.shape))
    beside = place[:longest] + [(place[longest] + 1) % drawn.shape[longest]] + place[longest + 1:]
    return drawn.at[tuple(place)].set(least).at[tuple(beside)].set(largest)


def raised(array, own_key, source, target, parts, factor):
    def block_of(axis_at):
        return (jnp.arange(array.shape[axis_at]) // (array.shape[axis_at] // parts)).reshape((-1,) + (1,) * (array.ndim - 1 - axis_at))

    first = jax.random.permutation(own_key, parts)[block_of(target)]
    second = (block_of(target) + parts // 2) % parts
    return jnp.where((block_of(source) == first) | (block_of(source) == second), factor * array, array)


def levels(stream_key, shape, cuts, smallest, high):
    level, own = 1.0, jax.random.fold_in(stream_key, 6)
    for axis_at, parts in cuts:
        steps = jnp.exp(jax.random.uniform(jax.random.fold_in(own, axis_at), (parts,), jnp.float32, smallest / len(cuts), high / len(cuts)))
        level = level * jnp.repeat(steps, shape[axis_at] // parts).reshape([-1 if axis == axis_at else 1 for axis in range(len(shape))])
    return level


def noise(stream_key, dims, deviation, bound, cuts=(), held_as=jnp.bfloat16):
    loudness = levels(stream_key, dims, cuts, -0.22, 0.18) if cuts else 1.0
    entries = jax.random.normal(stream_key, dims, jnp.float32) * deviation * loudness
    return jnp.minimum(jnp.maximum(entries, -bound), bound).astype(held_as)


def bell_draw_with(own_key, dims, width, limit, cuts, heavy, held_as=jnp.bfloat16):
    values = width * jax.random.normal(own_key, dims, jnp.float32)
    if cuts:
        values = values * levels(own_key, dims, cuts, -0.22, 0.18)
    return jnp.clip(raised(values, jax.random.fold_in(own_key, 3), *heavy), -limit, limit).astype(held_as)


def setup_inputs(seed: int = 0) -> dict:
    arg_keys = jax.random.split(jax.random.key(seed), 10)
    return {
        "user_factors": noise(arg_keys[0], (USERS, R), (R ** -0.25), 4.0, ((0, 64),), jnp.float32),
        "item_factors": noise(arg_keys[1], (ITEMS, R), (R ** -0.25), 4.0, ((0, 128),), jnp.float32),
        "user_accum": jnp.clip(jnp.exp(math.log(0.5) - 2.3025851 * jax.random.uniform(arg_keys[2], (USERS, R), jnp.float32) ** levels(arg_keys[2], (USERS, R), ((0, 64),), -0.2, 0.2)), 0.05, 0.5),
        "item_accum": jnp.clip(jnp.exp(math.log(0.5) - 2.3025851 * jax.random.uniform(arg_keys[3], (ITEMS, R), jnp.float32) ** levels(arg_keys[3], (ITEMS, R), ((0, 128),), -0.2, 0.2)), 0.05, 0.5),
        "ratings": bell_draw_with(arg_keys[4], (SLABS, GROUPS, TILE, TILE), 1.0, 16.0, ((0, 64), (1, 2)), (0, 1, 64, 4.0)),
        "masks": jnp.clip(jax.random.uniform(arg_keys[5], (SLABS, GROUPS, TILE, TILE), jnp.float32, -1.0, 1.0) * levels(arg_keys[5], (SLABS, GROUPS, TILE, TILE), ((0, 64), (1, 2)), -0.4, 0.0), -1.0, 1.0).astype(jnp.bfloat16),
        "tile_users": touch_ends(jax.random.randint(arg_keys[6], (SLABS, GROUPS), 0, USR_DEV // TILE), jax.random.fold_in(arg_keys[6], 1), 0, (USR_DEV // TILE) - 1).astype(jnp.int32),
        "tile_items": draw_tile_items(jax.random.fold_in(arg_keys[9], 71), 0),
        "tile_counts": draw_tile_counts(jax.random.fold_in(arg_keys[9], 71), 0),
    }


learn_rate = 0.5
weight_decay = 0.1

def adagrad(param, squares, grad):
    step_grad = grad / SLABS + weight_decay * param
    total = squares + step_grad * step_grad
    return param - learn_rate * step_grad / jnp.sqrt(total)

def reference(user_factors, item_factors, user_accum, item_accum, ratings, masks, tile_users, tile_items, tile_counts):
    user_low = user_factors.astype(jnp.bfloat16)
    item_low = item_factors.astype(jnp.bfloat16)
    group_total = SLABS * HALVES * SLABS
    rating_tile = ratings.reshape(group_total, SLOTS, TILE, TILE)
    weight_tile = masks.reshape(group_total, SLOTS, TILE, TILE)
    user_index = tile_users.reshape(group_total, SLOTS)
    item_index = tile_items.reshape(group_total, SLOTS)
    live_count = tile_counts.reshape(group_total)

    def group(g, carry):
        user_grad, item_grad = carry
        slab_index = (g // (HALVES * SLABS)).astype(jnp.int32)
        for slot in range(SLOTS):
            user_row = (slab_index * (USR_DEV // TILE) + user_index[g, slot]) * TILE
            item_row = item_index[g, slot] * TILE
            user_rows = lax.dynamic_slice(user_low, (user_row, jnp.int32(0)), (TILE, R))
            item_rows = lax.dynamic_slice(item_low, (item_row, jnp.int32(0)), (TILE, R))
            predicted = jnp.dot(user_rows, item_rows.T, preferred_element_type=jnp.float32)
            active = (slot < live_count[g]).astype(jnp.float32)
            observed = jnp.maximum(weight_tile[g, slot].astype(jnp.float32), 0.0)
            residual = (active * observed * (predicted - rating_tile[g, slot].astype(jnp.float32))).astype(jnp.bfloat16)
            user_part = jnp.dot(residual, item_rows, preferred_element_type=jnp.float32)
            item_part = jnp.dot(residual.T, user_rows, preferred_element_type=jnp.float32)
            old_user = lax.dynamic_slice(user_grad, (user_row, jnp.int32(0)), (TILE, R))
            user_grad = lax.dynamic_update_slice(user_grad, old_user + user_part, (user_row, jnp.int32(0)))
            old_item = lax.dynamic_slice(item_grad, (item_row, jnp.int32(0)), (TILE, R))
            item_grad = lax.dynamic_update_slice(item_grad, old_item + item_part, (item_row, jnp.int32(0)))
        return (user_grad, item_grad)
    start = (jnp.zeros(user_factors.shape, jnp.float32), jnp.zeros(item_factors.shape, jnp.float32))
    user_grad, item_grad = lax.fori_loop(0, group_total, group, start)
    new_users = adagrad(user_factors, user_accum, user_grad)
    new_items = adagrad(item_factors, item_accum, item_grad)
    return (new_users, new_items)
```

```python
import jax
import jax.numpy as jnp
from jax import lax
from jax.experimental import pallas as pl
from jax.experimental.pallas import tpu as pltpu
from jax.sharding import PartitionSpec as P

learn_rate = 0.5
weight_decay = 0.1
TILE = 128
SLOTS = 4
CHUNK = 4


def adagrad(param, squares, grad, num_slabs):
    step_grad = grad / num_slabs + weight_decay * param
    total = squares + step_grad * step_grad
    return param - learn_rate * step_grad / jnp.sqrt(total)


def core_swap(block):
    devices = range(lax.axis_size("blk"))
    return lax.ppermute(block, "blk", [(i, i ^ 1) for i in devices])


def tile_kernel(
    core_ref,
    live_ref,
    users_ref,
    items_ref,
    own_ratings,
    own_masks,
    far_ratings,
    far_masks,
    item_rows,
    user_rows,
    user_cols,
    item_grad,
    user_grad,
    ratings,
    masks,
    sems,
):
    owners = item_rows.shape[0]
    chunks = owners // CHUNK
    core = core_ref[0]

    def copies(k):
        at = pl.ds(k * CHUNK, CHUNK)
        near, far = pl.ds(0, SLOTS), pl.ds(SLOTS, SLOTS)
        pairs = (
            (own_ratings.at[at, core], ratings.at[at, near]),
            (own_masks.at[at, core], masks.at[at, near]),
            (far_ratings.at[at], ratings.at[at, far]),
            (far_masks.at[at], masks.at[at, far]),
        )
        return [
            pltpu.make_async_copy(source, target, sems.at[k, i])
            for i, (source, target) in enumerate(pairs)
        ]

    for k in range(chunks):
        for copy in copies(k):
            copy.start()
    user_grad[...] = jnp.zeros_like(user_grad)

    def group(g, live_near, tiles):
        rows = item_rows[g]
        places = []
        for t in range(tiles):
            slot = jnp.where(t < live_near, t, t - live_near + SLOTS)
            block = users_ref[g * 2 * SLOTS + slot]
            within = items_ref[g * 2 * SLOTS + slot]
            places.append((slot, block, within))
        picked = jnp.concatenate([user_rows[block] for _, block, _ in places], 0)
        predicted = lax.dot_general(
            picked, rows, (((1,), (1,)), ((), ())), preferred_element_type=jnp.float32
        )
        wide = []
        for t, (slot, _, within) in enumerate(places):
            part = predicted[t * TILE : (t + 1) * TILE]
            second = within == 1
            chosen = jnp.where(second, part[:, TILE:], part[:, :TILE])
            observed = jnp.maximum(masks[g, slot].astype(jnp.float32), 0.0)
            residual = observed * (chosen - ratings[g, slot].astype(jnp.float32))
            wide.append(
                jnp.concatenate(
                    [jnp.where(second, 0.0, residual), jnp.where(second, residual, 0.0)], 1
                ).astype(jnp.bfloat16)
            )
        wide = jnp.concatenate(wide, 0)
        user_part = jnp.dot(wide, rows, preferred_element_type=jnp.float32)
        for t, (_, block, _) in enumerate(places):
            user_grad[block] += user_part[t * TILE : (t + 1) * TILE]
        turned = jnp.concatenate([user_cols[block] for _, block, _ in places], 1)
        item_grad[g] = jnp.dot(turned, wide, preferred_element_type=jnp.float32).astype(
            item_grad.dtype
        )

    def chunk(k, carry):
        for copy in copies(k):
            copy.wait()

        def one(i, carry):
            g = k * CHUNK + i
            live_near = live_ref[2 * g]
            live = live_near + live_ref[2 * g + 1]
            for tiles in range(2, 2 * SLOTS + 1):
                pl.when(live == tiles)(lambda tiles=tiles: group(g, live_near, tiles))
            return carry

        return lax.fori_loop(0, CHUNK, one, carry)

    lax.fori_loop(0, chunks, chunk, 0)


def tile_terms(
    core, live, users, items, ratings, masks, far_ratings, far_masks, item_rows, user_rows
):
    owners, rows, columns = item_rows.shape
    blocks = user_rows.shape[0]
    smem = pl.BlockSpec(memory_space=pltpu.SMEM)
    vmem = pl.BlockSpec(memory_space=pltpu.VMEM)
    far = pl.BlockSpec(memory_space=pl.ANY)
    return pl.pallas_call(
        tile_kernel,
        out_shape=(
            jax.ShapeDtypeStruct((owners, columns, rows), jnp.bfloat16),
            jax.ShapeDtypeStruct((blocks, TILE, columns), jnp.float32),
        ),
        in_specs=[smem] * 4 + [far] * 4 + [vmem] * 3,
        out_specs=(vmem, vmem),
        scratch_shapes=[
            pltpu.VMEM((owners, 2 * SLOTS, TILE, TILE), jnp.bfloat16),
            pltpu.VMEM((owners, 2 * SLOTS, TILE, TILE), jnp.bfloat16),
            pltpu.SemaphoreType.DMA((owners // CHUNK, 4)),
        ],
        compiler_params=pltpu.CompilerParams(vmem_limit_bytes=50 << 20),
        cost_estimate=pl.CostEstimate(
            flops=6 * owners * 5 * TILE * rows * columns,
            bytes_accessed=32 << 20,
            transcendentals=0,
        ),
    )(
        core,
        live.reshape(-1),
        users.reshape(-1),
        items.reshape(-1),
        ratings,
        masks,
        far_ratings,
        far_masks,
        item_rows,
        user_rows,
        user_rows.swapaxes(1, 2),
    )


def body(
    user_factors,
    item_factors,
    user_accum,
    item_accum,
    ratings,
    masks,
    tile_users,
    tile_items,
    tile_counts,
):
    num_slabs = lax.axis_size("blk")
    columns = user_factors.shape[1]
    owners = num_slabs // 2
    core = lax.axis_index("blk") % 2
    same_core = [[j for j in range(num_slabs) if j % 2 == c] for c in range(2)]

    item_low = item_factors.astype(jnp.bfloat16)
    user_low = user_factors.astype(jnp.bfloat16).reshape(-1, TILE, columns)
    blocks = user_low.shape[0]
    ratings = ratings.reshape(owners, 2, SLOTS, TILE, TILE)
    masks = masks.reshape(owners, 2, SLOTS, TILE, TILE)
    index = jnp.concatenate(
        [
            tile_counts.reshape(owners, 2, 1),
            tile_users.reshape(owners, 2, SLOTS),
            tile_items.reshape(owners, 2, SLOTS) % 2,
        ],
        2,
    )

    def split(array):
        return (
            lax.dynamic_index_in_dim(array, core, 1, keepdims=False),
            core_swap(lax.dynamic_index_in_dim(array, 1 - core, 1, keepdims=False)),
        )

    near, far = split(index)
    live = jnp.stack([near[:, 0], far[:, 0]], 1)
    users = jnp.concatenate([near[:, 1 : 1 + SLOTS], far[:, 1 : 1 + SLOTS] + blocks], 1)
    items = jnp.concatenate([near[:, 1 + SLOTS :], far[:, 1 + SLOTS :]], 1)
    far_ratings = split(ratings)[1]
    far_masks = split(masks)[1]
    user_rows = jnp.concatenate([user_low, core_swap(user_low)], 0)

    item_rows = lax.all_to_all(
        jnp.broadcast_to(item_low, (owners,) + item_low.shape),
        "blk",
        0,
        0,
        axis_index_groups=same_core,
        tiled=True,
    )
    item_grad, user_grad = tile_terms(
        core[None].astype(jnp.int32),
        live,
        users,
        items,
        ratings,
        masks,
        far_ratings,
        far_masks,
        item_rows,
        user_rows,
    )
    far_grad = core_swap(user_grad[blocks:].astype(jnp.bfloat16))
    half = (user_grad[:blocks] + far_grad.astype(jnp.float32)).astype(jnp.bfloat16)
    other = lax.ppermute(half, "rep", [(0, 1), (1, 0)])
    user_sum = half.astype(jnp.float32) + other.astype(jnp.float32)
    item_parts = lax.all_to_all(
        item_grad, "blk", 0, 0, axis_index_groups=same_core, tiled=True
    )
    item_sum = jnp.sum(item_parts.astype(jnp.float32), 0).T
    new_users = adagrad(user_factors, user_accum, user_sum.reshape(user_factors.shape), num_slabs)
    new_items = adagrad(item_factors, item_accum, item_sum, num_slabs)
    return (new_users, new_items)


def solution(mesh):
    in_specs = (
        P("blk", None),
        P(("blk", "rep"), None),
        P("blk", None),
        P(("blk", "rep"), None),
        P("blk", "rep", None, None),
        P("blk", "rep", None, None),
        P("blk", "rep"),
        P("blk", "rep"),
        P("blk", "rep"),
    )
    out_specs = (P("blk", None), P(("blk", "rep"), None))
    return jax.shard_map(body, mesh=mesh, in_specs=in_specs, out_specs=out_specs, check_vma=False)
```

```python
import jax
import jax.numpy as jnp
from jax import lax
from jax.experimental import pallas as pl
from jax.experimental.pallas import tpu as pltpu
from jax.sharding import PartitionSpec as P

learn_rate = 0.5
weight_decay = 0.1
TILE = 128
SLOTS = 4
XS, YS, ZS, CORES = 2, 4, 4, 2
RING = 4
HALF = RING // 2
PAIR = 2


def place(index):
    return (
        index // (YS * ZS * CORES),
        index // (ZS * CORES) % YS,
        index // CORES % ZS,
        index % CORES,
    )


def moved(index, way):
    at = [(a + d) % n for a, d, n in zip(place(index), way, (XS, YS, ZS, CORES))]
    return ((at[0] * YS + at[1]) * ZS + at[2]) * CORES + at[3]


def fetch(block, x=0, y=0, z=0, core=0):
    count = XS * YS * ZS * CORES
    route = [(moved(i, (x, y, z, core)), i) for i in range(count)]
    return lax.ppermute(block, "blk", route)


def adagrad(param, squares, grad, num_slabs):
    step_grad = grad / num_slabs + weight_decay * param
    total = squares + step_grad * step_grad
    return param - learn_rate * step_grad / jnp.sqrt(total)


def owner_at(here, part, step, lane):
    x, y, z, _ = here
    if part == 0:
        return (x * YS + (y + lane) % YS) * ZS + (z + step) % ZS
    return ((1 - x) * YS + (y + step) % YS) * ZS + (z + lane) % ZS


def tile_kernel(pieces, outs, *refs):
    size = len(pieces)
    device_ref, near_ref, far_ref, own_ratings, own_masks = refs[:5]
    far_tiles = refs[5]
    item_rows = refs[6 : 6 + size]
    user_rows, user_cols = refs[6 + size : 8 + size]
    item_out = refs[8 + size : 8 + size + len(outs)]
    user_grad = refs[8 + size + len(outs)]
    owners_ref, rows_ref, grads_ref, ratings, masks, tile_sems, row_sems, out_sems = refs[
        9 + size + len(outs) :
    ]
    here = place(device_ref[0])
    core = here[3]
    blocks = user_rows.shape[0] // 2
    item_at = own_ratings.shape[0] * CORES * SLOTS
    count_at = 2 * item_at
    plane_size = YS * ZS
    total = rows_ref.shape[0]

    def tile_copies(n, far_of):
        owner = owners_ref[n]
        near, far = pl.ds(0, SLOTS), pl.ds(SLOTS, SLOTS)
        pairs = (
            (own_ratings.at[owner, core], ratings.at[n, near]),
            (own_masks.at[owner, core], masks.at[n, near]),
            (far_tiles.at[far_of, 0, owner % plane_size], ratings.at[n, far]),
            (far_tiles.at[far_of, 1, owner % plane_size], masks.at[n, far]),
        )
        return [
            pltpu.make_async_copy(source, target, tile_sems.at[n, i])
            for i, (source, target) in enumerate(pairs)
        ]

    row_copies, at = [], 0
    for a, (part, step, first, lanes) in enumerate(pieces):
        row_copies.append(
            pltpu.make_async_copy(item_rows[a], rows_ref.at[pl.ds(at, lanes)], row_sems.at[a])
        )
        row_copies[-1].start()
        for lane in range(lanes):
            owners_ref[at + lane] = owner_at(here, part, step, first + lane)
            for copy in tile_copies(at + lane, part):
                copy.start()
        at += lanes
    out_copies = [
        pltpu.make_async_copy(grads_ref.at[pl.ds(b * RING, RING)], item_out[b], out_sems.at[b])
        for b in range(len(outs))
    ]
    user_grad[...] = jnp.zeros_like(user_grad)
    for copy in row_copies:
        copy.wait()

    def predict(n, live, tiles):
        rows = rows_ref[n]
        first = (owners_ref[n] * CORES + core) * SLOTS
        places = []
        for t in range(tiles):
            far = t >= live[0]
            slot = jnp.where(far, jnp.minimum(t - live[0], SLOTS - 1), t)
            at = first + slot
            block = jnp.where(far, far_ref[0, at] + blocks, near_ref[0, at])
            within = jnp.where(far, far_ref[0, item_at + at], near_ref[0, item_at + at]) % 2
            alive = t < live[0] + live[1]
            places.append((jnp.where(far, slot + SLOTS, slot), block, within, alive))
        picked = jnp.concatenate([user_rows[block] for _, block, _, _ in places], 0)
        predicted = lax.dot_general(
            picked, rows, (((1,), (1,)), ((), ())), preferred_element_type=jnp.float32
        )
        return places, rows, predicted

    def residuals(n, places, predicted):
        wide = []
        for t, (slot, _, within, alive) in enumerate(places):
            part = predicted[t * TILE : (t + 1) * TILE]
            second = within == 1
            chosen = jnp.where(second, part[:, TILE:], part[:, :TILE])
            observed = jnp.maximum(masks[n, slot].astype(jnp.float32), 0.0)
            residual = observed * (chosen - ratings[n, slot].astype(jnp.float32))
            residual = residual.astype(jnp.bfloat16)
            none = jnp.zeros_like(residual)
            low = jnp.where(jnp.logical_and(alive, within == 0), residual, none)
            high = jnp.where(jnp.logical_and(alive, second), residual, none)
            wide.append(jnp.concatenate([low, high], 1))
        return jnp.concatenate(wide, 0)

    def together(entries, lives, tiles):
        firsts = [predict(n, live, tiles) for n, live in zip(entries, lives)]
        wides = [
            residuals(n, places, predicted)
            for n, (places, _, predicted) in zip(entries, firsts)
        ]
        user_parts = []
        for n, (places, rows, _), wide in zip(entries, firsts, wides):
            user_parts.append(jnp.dot(wide, rows, preferred_element_type=jnp.float32))
            turned = jnp.concatenate([user_cols[block] for _, block, _, _ in places], 1)
            grads_ref[n] = jnp.dot(turned, wide, preferred_element_type=jnp.float32).astype(
                jnp.bfloat16
            )
        for (places, _, _), user_part in zip(firsts, user_parts):
            for t, (_, block, _, _) in enumerate(places):
                user_grad[block] += user_part[t * TILE : (t + 1) * TILE]

    def some(i, carry):
        entries = [i * PAIR + k for k in range(PAIR)]
        lives = []
        for n in entries:
            for copy in tile_copies(n, 0):
                copy.wait()
            at = count_at + owners_ref[n] * CORES + core
            lives.append((near_ref[0, at], far_ref[0, at]))
        most = jnp.maximum(*[live[0] + live[1] for live in lives])
        for tiles in range(2, 2 * SLOTS + 1):
            pl.when(most == tiles)(lambda tiles=tiles: together(entries, lives, tiles))
        for b, copy in enumerate(out_copies):
            pl.when(i == (b + 1) * (RING // PAIR) - 1)(copy.start)
        return carry

    lax.fori_loop(0, total // PAIR, some, 0)
    for copy in out_copies:
        copy.wait()


def tile_terms(pieces, outs, device, near, far, own_tiles, far_tiles, item_rows, user_rows, user_cols):
    _, rows, columns = item_rows[0].shape
    blocks = user_rows.shape[0]
    total = sum(piece[3] for piece in pieces)
    smem = pl.BlockSpec(memory_space=pltpu.SMEM)
    vmem = pl.BlockSpec(memory_space=pltpu.VMEM)
    hbm = pl.BlockSpec(memory_space=pltpu.HBM)
    anywhere = pl.BlockSpec(memory_space=pl.ANY)

    def kernel(*refs):
        tile_kernel(pieces, outs, *refs)

    result = pl.pallas_call(
        kernel,
        out_shape=[jax.ShapeDtypeStruct((RING, columns, rows), jnp.bfloat16)] * len(outs)
        + [jax.ShapeDtypeStruct((blocks, TILE, columns), jnp.float32)],
        in_specs=[smem] * 3 + [hbm] * 2 + [anywhere] * (1 + len(pieces)) + [vmem] * 2,
        out_specs=[anywhere] * len(outs) + [vmem],
        scratch_shapes=[
            pltpu.SMEM((total,), jnp.int32),
            pltpu.VMEM((total, rows, columns), jnp.bfloat16),
            pltpu.VMEM((total, columns, rows), jnp.bfloat16),
            pltpu.VMEM((total, 2 * SLOTS, TILE, TILE), jnp.bfloat16),
            pltpu.VMEM((total, 2 * SLOTS, TILE, TILE), jnp.bfloat16),
            pltpu.SemaphoreType.DMA((total, 4)),
            pltpu.SemaphoreType.DMA((len(pieces),)),
            pltpu.SemaphoreType.DMA((len(outs),)),
        ],
        compiler_params=pltpu.CompilerParams(vmem_limit_bytes=32 << 20),
        cost_estimate=pl.CostEstimate(
            flops=total * (3 << 28), bytes_accessed=total << 20, transcendentals=0
        ),
    )(device, near, far, *own_tiles, far_tiles, *item_rows, user_rows, user_cols)
    return result[: len(outs)], result[len(outs)]


def in_hbm(array):
    return pltpu.with_memory_space_constraint(array, pltpu.HBM)


def pack_kernel(device_ref, ratings, masks, out, sems):
    x, _, _, core = place(device_ref[0])
    copies = [
        pltpu.make_async_copy(
            array.at[plane, :, 1 - core], out.at[part, kind], sems.at[part, kind]
        )
        for part, plane in enumerate((x, 1 - x))
        for kind, array in enumerate((ratings, masks))
    ]
    for copy in copies:
        copy.start()
    for copy in copies:
        copy.wait()


def packed_tiles(device, ratings, masks):
    lanes = YS * ZS
    shape = (XS, lanes, CORES, SLOTS, TILE, TILE)
    hbm = pl.BlockSpec(memory_space=pltpu.HBM)
    return pl.pallas_call(
        pack_kernel,
        out_shape=jax.ShapeDtypeStruct((2, 2, lanes, SLOTS, TILE, TILE), jnp.bfloat16),
        in_specs=[pl.BlockSpec(memory_space=pltpu.SMEM), hbm, hbm],
        out_specs=pl.BlockSpec(memory_space=pltpu.VMEM),
        scratch_shapes=[pltpu.SemaphoreType.DMA((2, 2))],
        compiler_params=pltpu.CompilerParams(vmem_limit_bytes=16 << 20),
        cost_estimate=pl.CostEstimate(flops=0, bytes_accessed=16 << 20, transcendentals=0),
    )(device, *[in_hbm(array.reshape(shape)) for array in (ratings, masks)])


def added(*terms):
    return sum(term.astype(jnp.float32) for term in terms)


def body(
    user_factors,
    item_factors,
    user_accum,
    item_accum,
    ratings,
    masks,
    tile_users,
    tile_items,
    tile_counts,
):
    low = jnp.bfloat16
    num_slabs = lax.axis_size("blk")
    columns = user_factors.shape[1]
    owners = num_slabs // CORES
    device = lax.axis_index("blk")

    item_low = item_factors.astype(low)
    own_line = [item_low] + [fetch(item_low, y=d) for d in range(1, RING)]
    far_line = [fetch(item_low, x=1, z=d) for d in range(RING)]

    near = jnp.concatenate([tile_users, tile_items, tile_counts], 1)
    far = fetch(near, core=1)
    user_low = user_factors.astype(low).reshape(-1, TILE, columns)
    blocks = user_low.shape[0]
    far_rows = fetch(user_low, core=1)
    start, far, far_rows = lax.optimization_barrier((device[None], far, far_rows))
    packed = packed_tiles(start, ratings, masks)
    user_rows = jnp.concatenate([user_low, far_rows], 0)

    far_tiles = fetch(packed, core=1)
    own_line, far_line, user_rows = lax.optimization_barrier((own_line, far_line, user_rows))
    user_cols = user_rows.swapaxes(1, 2)
    rows = [jnp.stack(own_line), jnp.stack(far_line)]
    ahead = [fetch(rows[0], z=1), fetch(rows[1], y=1)]
    behind = [fetch(rows[0], z=-1), fetch(rows[1], y=-1)]

    def terms(pieces, outs, item_rows):
        return tile_terms(
            pieces,
            outs,
            device[None],
            near,
            far,
            [in_hbm(a.reshape(owners, CORES, SLOTS, TILE, TILE)) for a in (ratings, masks)],
            far_tiles,
            item_rows,
            user_rows,
            user_cols,
        )

    here_terms, user_first = terms(
        ((0, 0, 0, RING), (1, 0, 0, RING)), ((0, 0), (1, 0)), rows
    )
    ahead, behind, here_terms, user_first = lax.optimization_barrier(
        (ahead, behind, here_terms, user_first)
    )
    across = [
        [fetch(ahead[0][:HALF], z=1), fetch(behind[0][HALF:], z=-1)],
        [fetch(ahead[1][:HALF], y=1), fetch(behind[1][HALF:], y=-1)],
    ]
    near_terms, user_second = terms(
        ((0, 1, 0, RING), (1, 1, 0, RING), (0, 3, 0, RING), (1, 3, 0, RING)),
        ((0, 1), (1, 1), (0, 3), (1, 3)),
        [ahead[0], ahead[1], behind[0], behind[1]],
    )
    across_terms, user_third = terms(
        ((0, 2, 0, HALF), (0, 2, HALF, HALF), (1, 2, 0, HALF), (1, 2, HALF, HALF)),
        ((0, 2), (1, 2)),
        across[0] + across[1],
    )

    arrived = [
        [fetch(near_terms[0], z=-1), fetch(near_terms[2], z=1)],
        [fetch(near_terms[1], y=-1), fetch(near_terms[3], y=1)],
    ]
    arrived, across_terms = lax.optimization_barrier((arrived, across_terms))

    def user_part(begin):
        return added(*[g[begin : begin + blocks] for g in (user_first, user_second, user_third)])

    far_grad = fetch(user_part(blocks).astype(low), core=1)
    half = (user_part(0) + far_grad.astype(jnp.float32)).astype(low)

    def lines(mine, arrived):
        return [added(mine[k], *[a[k] for a in arrived]).astype(low) for k in range(RING)]

    own_sum = lines(here_terms[0], arrived[0] + [fetch(across_terms[0], z=2)])
    far_sum = lines(here_terms[1], arrived[1] + [fetch(across_terms[1], y=2)])
    other = lax.ppermute(half, "rep", [(0, 1), (1, 0)])
    own_sum, far_sum, other = lax.optimization_barrier((own_sum, far_sum, other))
    user_sum = added(half, other)
    item_sum = added(
        own_sum[0],
        *[fetch(own_sum[d], y=-d) for d in range(1, RING)],
        *[fetch(far_sum[d], x=1, z=-d) for d in range(RING)],
    ).T
    new_users = adagrad(user_factors, user_accum, user_sum.reshape(user_factors.shape), num_slabs)
    new_items = adagrad(item_factors, item_accum, item_sum, num_slabs)
    return (new_users, new_items)


def solution(mesh):
    in_specs = (
        P("blk", None),
        P(("blk", "rep"), None),
        P("blk", None),
        P(("blk", "rep"), None),
        P("blk", "rep", None, None),
        P("blk", "rep", None, None),
        P("blk", "rep"),
        P("blk", "rep"),
        P("blk", "rep"),
    )
    out_specs = (P("blk", None), P(("blk", "rep"), None))
    return jax.shard_map(body, mesh=mesh, in_specs=in_specs, out_specs=out_specs, check_vma=False)
```

```python
import jax
import jax.numpy as jnp
from jax import lax
from jax.experimental import pallas as pl
from jax.experimental.pallas import tpu as pltpu
from jax.sharding import PartitionSpec as P

learn_rate = 0.5
weight_decay = 0.1
TILE = 128
SLOTS = 4
XS, YS, ZS, CORES = 2, 4, 4, 2
RING = 4
PAIR = 2


def place(index):
    return (
        index // (YS * ZS * CORES),
        index // (ZS * CORES) % YS,
        index // CORES % ZS,
        index % CORES,
    )


def moved(index, way):
    at = [(a + d) % n for a, d, n in zip(place(index), way, (XS, YS, ZS, CORES))]
    return ((at[0] * YS + at[1]) * ZS + at[2]) * CORES + at[3]


def fetch(block, x=0, y=0, z=0, core=0):
    count = XS * YS * ZS * CORES
    route = [(moved(i, (x, y, z, core)), i) for i in range(count)]
    return lax.ppermute(block, "blk", route)


def exchange_along_y(blocks):
    lines = [
        [((x * YS + y) * ZS + z) * CORES + core for y in range(YS)]
        for x in range(XS)
        for z in range(ZS)
        for core in range(CORES)
    ]
    return lax.all_to_all(blocks, "blk", 0, 0, axis_index_groups=lines, tiled=True)


def adagrad(param, squares, grad, num_slabs):
    step_grad = grad / num_slabs + weight_decay * param
    total = squares + step_grad * step_grad
    return param - learn_rate * step_grad / jnp.sqrt(total)


def owner_at(here, part, step, lane):
    x, y, z, _ = here
    if part == 0:
        return (x * YS + lane) * ZS + (z + step) % ZS
    return ((1 - x) * YS + (y + step) % YS) * ZS + (z + lane) % ZS


def tile_kernel(pieces, outs, *refs):
    size = len(pieces)
    device_ref, near_ref, far_ref, near_live, far_live, own_ratings, own_masks = refs[:7]
    far_ratings, far_masks = refs[7:9]
    item_rows = refs[9 : 9 + size]
    user_rows, user_cols, user_before = refs[9 + size : 12 + size]
    item_out = refs[12 + size : 12 + size + len(outs)]
    user_grad = refs[12 + size + len(outs)]
    owners_ref, rows_ref, grads_ref, ratings, masks, tile_sems, row_sems, out_sems = refs[
        13 + size + len(outs) :
    ]
    here = place(device_ref[0])
    core = here[3]
    blocks = user_rows.shape[0] // 2
    total = rows_ref.shape[0]

    def tile_copies(n):
        owner = owners_ref[n]
        near, far = pl.ds(0, SLOTS), pl.ds(SLOTS, SLOTS)
        pairs = (
            (own_ratings.at[owner, core], ratings.at[n, near]),
            (own_masks.at[owner, core], masks.at[n, near]),
            (far_ratings.at[owner, core], ratings.at[n, far]),
            (far_masks.at[owner, core], masks.at[n, far]),
        )
        return [
            pltpu.make_async_copy(source, target, tile_sems.at[n, i])
            for i, (source, target) in enumerate(pairs)
        ]

    row_copies, at = [], 0
    for a, (part, step, first, lanes) in enumerate(pieces):
        row_copies.append(
            pltpu.make_async_copy(item_rows[a], rows_ref.at[pl.ds(at, lanes)], row_sems.at[a])
        )
        row_copies[-1].start()
        for lane in range(lanes):
            owners_ref[at + lane] = owner_at(here, part, step, first + lane)
            for copy in tile_copies(at + lane):
                copy.start()
        at += lanes
    out_copies = [
        pltpu.make_async_copy(grads_ref.at[pl.ds(b * RING, RING)], item_out[b], out_sems.at[b])
        for b in range(len(outs))
    ]
    if user_before is None:
        user_grad[...] = jnp.zeros_like(user_grad)
    else:
        row_copies.append(pltpu.make_async_copy(user_before, user_grad, row_sems.at[size]))
        row_copies[-1].start()
    for copy in row_copies:
        copy.wait()

    def predict(n, live, tiles):
        rows = rows_ref[n]
        first = (owners_ref[n] * CORES + core) * SLOTS
        places = []
        for t in range(tiles):
            far = t >= live[0]
            slot = jnp.where(far, jnp.minimum(t - live[0], SLOTS - 1), t)
            at = first + slot
            code = jnp.where(far, far_ref[0, at] + 2 * blocks, near_ref[0, at])
            block, within = code // 2, code % 2
            alive = t < live[0] + live[1]
            places.append((jnp.where(far, slot + SLOTS, slot), block, within, alive))
        picked = jnp.concatenate([user_rows[block] for _, block, _, _ in places], 0)
        predicted = lax.dot_general(
            picked, rows, (((1,), (1,)), ((), ())), preferred_element_type=jnp.float32
        )
        return places, rows, predicted

    def residuals(n, places, predicted):
        wide = []
        for t, (slot, _, within, alive) in enumerate(places):
            part = predicted[t * TILE : (t + 1) * TILE]
            second = within == 1
            chosen = jnp.where(second, part[:, TILE:], part[:, :TILE])
            observed = jnp.maximum(masks[n, slot].astype(jnp.float32), 0.0)
            residual = observed * (chosen - ratings[n, slot].astype(jnp.float32))
            residual = residual.astype(jnp.bfloat16)
            none = jnp.zeros_like(residual)
            low = jnp.where(jnp.logical_and(alive, within == 0), residual, none)
            high = jnp.where(jnp.logical_and(alive, second), residual, none)
            wide.append(jnp.concatenate([low, high], 1))
        return jnp.concatenate(wide, 0)

    def together(entries, lives, tiles):
        firsts = [predict(n, live, tiles) for n, live in zip(entries, lives)]
        wides = [
            residuals(n, places, predicted)
            for n, (places, _, predicted) in zip(entries, firsts)
        ]
        user_parts = []
        for n, (places, rows, _), wide in zip(entries, firsts, wides):
            user_parts.append(jnp.dot(wide, rows, preferred_element_type=jnp.float32))
            turned = jnp.concatenate([user_cols[block] for _, block, _, _ in places], 1)
            grads_ref[n] = jnp.dot(turned, wide, preferred_element_type=jnp.float32).astype(
                jnp.bfloat16
            )
        for (places, _, _), user_part in zip(firsts, user_parts):
            for t, (_, block, _, _) in enumerate(places):
                user_grad[block] += user_part[t * TILE : (t + 1) * TILE]

    def some(i, carry):
        entries = [i * PAIR + k for k in range(PAIR)]
        lives = []
        for n in entries:
            for copy in tile_copies(n):
                copy.wait()
            at = owners_ref[n] * CORES + core
            lives.append((near_live[0, at], far_live[0, at]))
        most = jnp.maximum(*[live[0] + live[1] for live in lives])
        for tiles in range(2, 2 * SLOTS + 1):
            pl.when(most == tiles)(lambda tiles=tiles: together(entries, lives, tiles))
        for b, copy in enumerate(out_copies):
            pl.when(i == (b + 1) * (RING // PAIR) - 1)(copy.start)
        return carry

    lax.fori_loop(0, total // PAIR, some, 0)
    for copy in out_copies:
        copy.wait()


def tile_terms(pieces, outs, device, indices, own_tiles, far_tiles, item_rows, user_rows, user_cols, user_before):
    _, rows, columns = item_rows[0].shape
    blocks = user_rows.shape[0]
    total = sum(piece[3] for piece in pieces)
    smem = pl.BlockSpec(memory_space=pltpu.SMEM)
    vmem = pl.BlockSpec(memory_space=pltpu.VMEM)
    hbm = pl.BlockSpec(memory_space=pltpu.HBM)
    anywhere = pl.BlockSpec(memory_space=pl.ANY)

    first = user_before is None

    def kernel(*refs):
        cut = 11 + len(pieces)
        tile_kernel(pieces, outs, *refs[:cut], *((None,) if first else ()), *refs[cut:])

    result = pl.pallas_call(
        kernel,
        out_shape=[jax.ShapeDtypeStruct((RING, columns, rows), jnp.bfloat16)] * len(outs)
        + [jax.ShapeDtypeStruct((blocks, TILE, columns), jnp.float32)],
        in_specs=[smem] * 5 + [hbm] * 4 + [anywhere] * len(pieces) + [vmem] * 2
        + [anywhere] * (not first),
        out_specs=[anywhere] * len(outs) + [vmem],
        scratch_shapes=[
            pltpu.SMEM((total,), jnp.int32),
            pltpu.VMEM((total, rows, columns), jnp.bfloat16),
            pltpu.VMEM((total, columns, rows), jnp.bfloat16),
            pltpu.VMEM((total, 2 * SLOTS, TILE, TILE), jnp.bfloat16),
            pltpu.VMEM((total, 2 * SLOTS, TILE, TILE), jnp.bfloat16),
            pltpu.SemaphoreType.DMA((total, 4)),
            pltpu.SemaphoreType.DMA((len(pieces) + 1,)),
            pltpu.SemaphoreType.DMA((len(outs),)),
        ],
        compiler_params=pltpu.CompilerParams(vmem_limit_bytes=32 << 20),
        cost_estimate=pl.CostEstimate(
            flops=total * (3 << 28), bytes_accessed=total << 20, transcendentals=0
        ),
    )(device, *indices, *own_tiles, *far_tiles, *item_rows, user_rows, user_cols, *(() if first else (user_before,)))
    return result[: len(outs)], result[len(outs)]


def in_hbm(array):
    return pltpu.with_memory_space_constraint(array, pltpu.HBM)


def added(*terms):
    return sum(term.astype(jnp.float32) for term in terms)


def body(
    user_factors,
    item_factors,
    user_accum,
    item_accum,
    ratings,
    masks,
    tile_users,
    tile_items,
    tile_counts,
):
    low = jnp.bfloat16
    num_slabs = lax.axis_size("blk")
    columns = user_factors.shape[1]
    owners = num_slabs // CORES
    device = lax.axis_index("blk")

    near = tile_users * 2 + tile_items % 2
    far, far_live = fetch(near, core=1), fetch(tile_counts, core=1)
    user_low = user_factors.astype(low).reshape(-1, TILE, columns)
    blocks = user_low.shape[0]
    far_rows = fetch(user_low, core=1)
    item_low = item_factors.astype(low)
    cross = fetch(item_low, x=1)
    shape = (owners, CORES, SLOTS, TILE, TILE)
    own_tiles = [ratings.reshape(shape), masks.reshape(shape)]
    first, second, cross, far, far_live, far_rows = lax.optimization_barrier(
        (*own_tiles, cross, far, far_live, far_rows)
    )
    far_tiles = [fetch(first, core=1), fetch(second, core=1)]
    user_rows = jnp.concatenate([user_low, far_rows], 0)

    own_line = exchange_along_y(jnp.broadcast_to(item_low, (YS,) + item_low.shape))
    far_line = [cross] + [fetch(cross, z=d) for d in range(1, RING)]
    own_line, far_line, user_rows, far_tiles[0] = lax.optimization_barrier(
        (own_line, far_line, user_rows, far_tiles[0])
    )
    user_cols = user_rows.swapaxes(1, 2)
    rows = [own_line, jnp.stack(far_line)]
    ahead = [fetch(rows[0], z=1), fetch(rows[1], y=1)]
    behind = [fetch(rows[0], z=-1), fetch(rows[1], y=-1)]

    def terms(pieces, outs, item_rows, user_before):
        return tile_terms(
            pieces,
            outs,
            device[None],
            (near, far, tile_counts, far_live),
            [in_hbm(array) for array in own_tiles],
            [in_hbm(array) for array in far_tiles],
            item_rows,
            user_rows,
            user_cols,
            user_before,
        )

    here_terms, user_first = terms(
        ((0, 0, 0, RING), (1, 0, 0, RING)), ((0, 0), (1, 0)), rows, None
    )
    rows, ahead, behind, here_terms, user_first = lax.optimization_barrier(
        (rows, ahead, behind, here_terms, user_first)
    )
    across = [fetch(rows[0], z=2), fetch(rows[1], y=2)]
    near_terms, user_second = terms(
        ((0, 1, 0, RING), (1, 1, 0, RING), (0, 3, 0, RING), (1, 3, 0, RING)),
        ((0, 1), (1, 1), (0, 3), (1, 3)),
        [ahead[0], ahead[1], behind[0], behind[1]],
        user_first,
    )
    across_terms, user_grad = terms(
        ((0, 2, 0, RING), (1, 2, 0, RING)), ((0, 2), (1, 2)), across, user_second
    )
    arrived = [
        [fetch(near_terms[0], z=-1), fetch(near_terms[2], z=1)],
        [fetch(near_terms[1], y=-1), fetch(near_terms[3], y=1)],
    ]
    arrived, across_terms = lax.optimization_barrier((arrived, across_terms))

    far_grad = fetch(user_grad[blocks:].astype(low), core=1)
    half = (user_grad[:blocks] + far_grad.astype(jnp.float32)).astype(low)
    own_last, far_last = fetch(across_terms[0], z=2), fetch(across_terms[1], y=2)
    half, own_last, far_last = lax.optimization_barrier((half, own_last, far_last))
    other = lax.ppermute(half, "rep", [(0, 1), (1, 0)])
    user_sum = added(half, other)
    own_sum = added(here_terms[0], *arrived[0], own_last).astype(low)
    far_sum = [
        added(here_terms[1][k], *[a[k] for a in arrived[1]], far_last[k]).astype(low)
        for k in range(RING)
    ]
    own_sum, far_sum = lax.optimization_barrier((own_sum, far_sum))
    cross_sum = added(far_sum[0], *[fetch(far_sum[d], z=-d) for d in range(1, RING)]).astype(low)
    cross_sum, other = lax.optimization_barrier((cross_sum, other))
    user_sum = added(half, other)
    item_sum = added(
        jnp.sum(exchange_along_y(own_sum).astype(jnp.float32), 0),
        fetch(cross_sum, x=1),
    ).T
    new_users = adagrad(user_factors, user_accum, user_sum.reshape(user_factors.shape), num_slabs)
    new_items = adagrad(item_factors, item_accum, item_sum, num_slabs)
    return (new_users, new_items)


def solution(mesh):
    in_specs = (
        P("blk", None),
        P(("blk", "rep"), None),
        P("blk", None),
        P(("blk", "rep"), None),
        P("blk", "rep", None, None),
        P("blk", "rep", None, None),
        P("blk", "rep"),
        P("blk", "rep"),
        P("blk", "rep"),
    )
    out_specs = (P("blk", None), P(("blk", "rep"), None))
    return jax.shard_map(body, mesh=mesh, in_specs=in_specs, out_specs=out_specs, check_vma=False)
```

```python
import jax
import jax.numpy as jnp
from jax import lax
from jax.experimental import pallas as pl
from jax.experimental.pallas import tpu as pltpu
from jax.sharding import PartitionSpec as P

learn_rate = 0.5
weight_decay = 0.1
TILE = 128
SLOTS = 4
XS, YS, ZS, CORES = 2, 4, 4, 2
RING = 4
PAIR = 2


def place(index):
    return (
        index // (YS * ZS * CORES),
        index // (ZS * CORES) % YS,
        index // CORES % ZS,
        index % CORES,
    )


def moved(index, way):
    at = [(a + d) % n for a, d, n in zip(place(index), way, (XS, YS, ZS, CORES))]
    return ((at[0] * YS + at[1]) * ZS + at[2]) * CORES + at[3]


def fetch(block, x=0, y=0, z=0, core=0):
    count = XS * YS * ZS * CORES
    route = [(moved(i, (x, y, z, core)), i) for i in range(count)]
    return lax.ppermute(block, "blk", route)


def exchange_along_y(blocks):
    lines = [
        [((x * YS + y) * ZS + z) * CORES + core for y in range(YS)]
        for x in range(XS)
        for z in range(ZS)
        for core in range(CORES)
    ]
    return lax.all_to_all(blocks, "blk", 0, 0, axis_index_groups=lines, tiled=True)


def adagrad(param, squares, grad, num_slabs):
    step_grad = grad / num_slabs + weight_decay * param
    total = squares + step_grad * step_grad
    return param - learn_rate * step_grad / jnp.sqrt(total)


def owner_at(here, part, step, lane):
    x, y, z, _ = here
    if part == 0:
        return (x * YS + (y + lane) % YS) * ZS + (z + step) % ZS
    return ((1 - x) * YS + (y + step) % YS) * ZS + (z + lane) % ZS


def tile_kernel(pieces, outs, last, *refs):
    size = len(pieces)
    device_ref, near_ref, far_ref, near_live, far_live, own_ratings, own_masks = refs[:7]
    far_ratings, far_masks = refs[7:9]
    item_rows = refs[9 : 9 + size]
    user_rows, user_cols, user_before = refs[9 + size : 12 + size]
    item_out = refs[12 + size : 12 + size + len(outs)]
    after = 12 + size + len(outs)
    if last:
        user_near, user_far = refs[after : after + 2]
        user_grad = refs[-1]
    else:
        user_grad = refs[after]
    after += 1 + last
    owners_ref, rows_ref, grads_ref, ratings, masks, tile_sems, row_sems, out_sems = refs[
        after : after + 8
    ]
    here = place(device_ref[0])
    core = here[3]
    blocks = user_rows.shape[0] // 2
    total = rows_ref.shape[0]

    def tile_copies(n):
        owner = owners_ref[n]
        near, far = pl.ds(0, SLOTS), pl.ds(SLOTS, SLOTS)
        pairs = (
            (own_ratings.at[owner, core], ratings.at[n, near]),
            (own_masks.at[owner, core], masks.at[n, near]),
            (far_ratings.at[owner, core], ratings.at[n, far]),
            (far_masks.at[owner, core], masks.at[n, far]),
        )
        return [
            pltpu.make_async_copy(source, target, tile_sems.at[n, i])
            for i, (source, target) in enumerate(pairs)
        ]

    row_copies, at = [], 0
    for a, (part, step, first, lanes) in enumerate(pieces):
        for lane in range(lanes):
            source = (here[1] + lane) % YS if part == 0 else lane
            row_copies.append(
                pltpu.make_async_copy(
                    item_rows[a].at[source], rows_ref.at[at + lane], row_sems.at[at + lane]
                )
            )
            row_copies[-1].start()
        for lane in range(lanes):
            owners_ref[at + lane] = owner_at(here, part, step, first + lane)
            for copy in tile_copies(at + lane):
                copy.start()
        at += lanes
    out_copies = [
        pltpu.make_async_copy(grads_ref.at[pl.ds(b * RING, RING)], item_out[b], out_sems.at[b])
        for b in range(len(outs))
    ]
    if user_before is None:
        user_grad[...] = jnp.zeros_like(user_grad)
    else:
        row_copies.append(pltpu.make_async_copy(user_before, user_grad, row_sems.at[total]))
        row_copies[-1].start()
    for copy in row_copies:
        copy.wait()

    def predict(n, live, tiles):
        rows = rows_ref[n]
        first = (owners_ref[n] * CORES + core) * SLOTS
        places = []
        for t in range(tiles):
            far = t >= live[0]
            slot = jnp.where(far, jnp.minimum(t - live[0], SLOTS - 1), t)
            at = first + slot
            code = jnp.where(far, far_ref[0, at] + 2 * blocks, near_ref[0, at])
            block, within = code // 2, code % 2
            alive = t < live[0] + live[1]
            places.append((jnp.where(far, slot + SLOTS, slot), block, within, alive))
        picked = jnp.concatenate([user_rows[block] for _, block, _, _ in places], 0)
        predicted = lax.dot_general(
            picked, rows, (((1,), (1,)), ((), ())), preferred_element_type=jnp.float32
        )
        return places, rows, predicted

    def residuals(n, places, predicted):
        wide = []
        for t, (slot, _, within, alive) in enumerate(places):
            part = predicted[t * TILE : (t + 1) * TILE]
            second = within == 1
            chosen = jnp.where(second, part[:, TILE:], part[:, :TILE])
            observed = jnp.maximum(masks[n, slot].astype(jnp.float32), 0.0)
            residual = observed * (chosen - ratings[n, slot].astype(jnp.float32))
            residual = residual.astype(jnp.bfloat16)
            none = jnp.zeros_like(residual)
            low = jnp.where(jnp.logical_and(alive, within == 0), residual, none)
            high = jnp.where(jnp.logical_and(alive, second), residual, none)
            wide.append(jnp.concatenate([low, high], 1))
        return jnp.concatenate(wide, 0)

    def together(entries, lives, tiles):
        firsts = [predict(n, live, tiles) for n, live in zip(entries, lives)]
        wides = [
            residuals(n, places, predicted)
            for n, (places, _, predicted) in zip(entries, firsts)
        ]
        user_parts = []
        for n, (places, rows, _), wide in zip(entries, firsts, wides):
            user_parts.append(jnp.dot(wide, rows, preferred_element_type=jnp.float32))
            turned = jnp.concatenate([user_cols[block] for _, block, _, _ in places], 1)
            grads_ref[n] = jnp.dot(turned, wide, preferred_element_type=jnp.float32).astype(
                jnp.bfloat16
            )
        for (places, _, _), user_part in zip(firsts, user_parts):
            for t, (_, block, _, _) in enumerate(places):
                user_grad[block] += user_part[t * TILE : (t + 1) * TILE]

    def some(i, carry):
        entries = [i * PAIR + k for k in range(PAIR)]
        lives = []
        for n in entries:
            for copy in tile_copies(n):
                copy.wait()
            at = owners_ref[n] * CORES + core
            lives.append((near_live[0, at], far_live[0, at]))
        most = jnp.maximum(*[live[0] + live[1] for live in lives])
        for tiles in range(2, 2 * SLOTS + 1):
            pl.when(most == tiles)(lambda tiles=tiles: together(entries, lives, tiles))
        for b, copy in enumerate(out_copies):
            pl.when(i == (b + 1) * (RING // PAIR) - 1)(copy.start)
        return carry

    lax.fori_loop(0, total // PAIR, some, 0)
    if last:
        user_near[...] = user_grad[pl.ds(0, blocks)]
        user_far[...] = user_grad[pl.ds(blocks, blocks)].astype(user_far.dtype)
    for copy in out_copies:
        copy.wait()


def tile_terms(pieces, outs, device, indices, own_tiles, far_tiles, item_rows, user_rows, user_cols, user_before, last):
    _, rows, columns = item_rows[0].shape
    blocks = user_rows.shape[0]
    total = sum(piece[3] for piece in pieces)
    smem = pl.BlockSpec(memory_space=pltpu.SMEM)
    vmem = pl.BlockSpec(memory_space=pltpu.VMEM)
    hbm = pl.BlockSpec(memory_space=pltpu.HBM)
    anywhere = pl.BlockSpec(memory_space=pl.ANY)

    first = user_before is None
    users = [jax.ShapeDtypeStruct((blocks, TILE, columns), jnp.float32)]
    if last:
        half = (blocks // 2, TILE, columns)
        users = [jax.ShapeDtypeStruct(half, jnp.float32), jax.ShapeDtypeStruct(half, jnp.bfloat16)]

    def kernel(*refs):
        cut = 11 + len(pieces)
        tile_kernel(pieces, outs, last, *refs[:cut], *((None,) if first else ()), *refs[cut:])

    result = pl.pallas_call(
        kernel,
        out_shape=[jax.ShapeDtypeStruct((RING, columns, rows), jnp.bfloat16)] * len(outs)
        + users,
        in_specs=[smem] * 5 + [hbm] * 4 + [anywhere] * len(pieces) + [vmem] * 2
        + [anywhere] * (not first),
        out_specs=[anywhere] * len(outs) + [vmem] * len(users),
        scratch_shapes=[
            pltpu.SMEM((total,), jnp.int32),
            pltpu.VMEM((total, rows, columns), jnp.bfloat16),
            pltpu.VMEM((total, columns, rows), jnp.bfloat16),
            pltpu.VMEM((total, 2 * SLOTS, TILE, TILE), jnp.bfloat16),
            pltpu.VMEM((total, 2 * SLOTS, TILE, TILE), jnp.bfloat16),
            pltpu.SemaphoreType.DMA((total, 4)),
            pltpu.SemaphoreType.DMA((total + 1,)),
            pltpu.SemaphoreType.DMA((len(outs),)),
        ]
        + [pltpu.VMEM((blocks, TILE, columns), jnp.float32)] * last,
        compiler_params=pltpu.CompilerParams(vmem_limit_bytes=(total + 12) << 20),
        cost_estimate=pl.CostEstimate(
            flops=total * (3 << 28), bytes_accessed=total << 20, transcendentals=0
        ),
    )(device, *indices, *own_tiles, *far_tiles, *item_rows, user_rows, user_cols, *(() if first else (user_before,)))
    return result[: len(outs)], result[len(outs) :]


def in_hbm(array):
    return pltpu.with_memory_space_constraint(array, pltpu.HBM)


def added(*terms):
    return sum(term.astype(jnp.float32) for term in terms)


def body(
    user_factors,
    item_factors,
    user_accum,
    item_accum,
    ratings,
    masks,
    tile_users,
    tile_items,
    tile_counts,
):
    low = jnp.bfloat16
    num_slabs = lax.axis_size("blk")
    columns = user_factors.shape[1]
    owners = num_slabs // CORES
    device = lax.axis_index("blk")

    near = tile_users * 2 + tile_items % 2
    far, far_live = fetch(near, core=1), fetch(tile_counts, core=1)
    user_low = user_factors.astype(low).reshape(-1, TILE, columns)
    blocks = user_low.shape[0]
    far_rows = fetch(user_low, core=1)
    item_low = item_factors.astype(low)
    cross = fetch(item_low, x=1)
    shape = (owners, CORES, SLOTS, TILE, TILE)
    own_tiles = [ratings.reshape(shape), masks.reshape(shape)]
    first, second, cross, far, far_live, far_rows = lax.optimization_barrier(
        (*own_tiles, cross, far, far_live, far_rows)
    )
    far_tiles = [fetch(first, core=1), fetch(second, core=1)]
    user_rows = jnp.concatenate([user_low, far_rows], 0)

    own_line = exchange_along_y(jnp.broadcast_to(item_low, (YS,) + item_low.shape))
    far_line = [cross] + [fetch(cross, z=d) for d in range(1, RING)]
    own_line, far_line, user_rows, far_tiles[0] = lax.optimization_barrier(
        (own_line, far_line, user_rows, far_tiles[0])
    )
    user_cols = user_rows.swapaxes(1, 2)
    rows = [own_line, jnp.stack(far_line)]
    ahead = [fetch(rows[0], z=1), fetch(rows[1], y=1)]
    behind = [fetch(rows[0], z=-1), fetch(rows[1], y=-1)]

    def terms(pieces, outs, item_rows, user_before, last=False):
        return tile_terms(
            pieces,
            outs,
            device[None],
            (near, far, tile_counts, far_live),
            [in_hbm(array) for array in own_tiles],
            [in_hbm(array) for array in far_tiles],
            item_rows,
            user_rows,
            user_cols,
            user_before,
            last,
        )

    here_terms, (user_first,) = terms(
        ((0, 0, 0, RING), (1, 0, 0, RING)), ((0, 0), (1, 0)), rows, None
    )
    rows, ahead, behind, here_terms, user_first = lax.optimization_barrier(
        (rows, ahead, behind, here_terms, user_first)
    )
    across = [fetch(rows[0], z=2), fetch(rows[1], y=2)]
    near_terms, (user_second,) = terms(
        ((0, 1, 0, RING), (1, 1, 0, RING), (0, 3, 0, RING), (1, 3, 0, RING)),
        ((0, 1), (1, 1), (0, 3), (1, 3)),
        [ahead[0], ahead[1], behind[0], behind[1]],
        user_first,
    )
    across_terms, (user_near, user_far) = terms(
        ((0, 2, 0, RING), (1, 2, 0, RING)), ((0, 2), (1, 2)), across, user_second, True
    )
    arrived = [
        [fetch(near_terms[0], z=-1), fetch(near_terms[2], z=1)],
        [fetch(near_terms[1], y=-1), fetch(near_terms[3], y=1)],
    ]
    far_grad = fetch(user_far, core=1)
    arrived, across_terms, far_grad = lax.optimization_barrier((arrived, across_terms, far_grad))
    half = (user_near + far_grad.astype(jnp.float32)).astype(low)
    arrived[0].append(fetch(across_terms[0], z=2))
    arrived[1].append(fetch(across_terms[1], y=2))
    other = lax.ppermute(half, "rep", [(0, 1), (1, 0)])

    def lines(part):
        return [
            added(here_terms[part][k], *[a[k] for a in arrived[part]]).astype(low)
            for k in range(RING)
        ]

    far_sum, own_sum = lines(1), lines(0)
    cross_sum = added(far_sum[0], *[fetch(far_sum[d], z=-d) for d in range(1, RING)]).astype(low)
    own_sum, other = lax.optimization_barrier((own_sum, other))
    user_sum = added(half, other)
    item_sum = added(
        own_sum[0],
        *[fetch(own_sum[d], y=-d) for d in range(1, RING)],
        fetch(cross_sum, x=1),
    ).T
    new_users = adagrad(user_factors, user_accum, user_sum.reshape(user_factors.shape), num_slabs)
    new_items = adagrad(item_factors, item_accum, item_sum, num_slabs)
    return (new_users, new_items)


def solution(mesh):
    in_specs = (
        P("blk", None),
        P(("blk", "rep"), None),
        P("blk", None),
        P(("blk", "rep"), None),
        P("blk", "rep", None, None),
        P("blk", "rep", None, None),
        P("blk", "rep"),
        P("blk", "rep"),
        P("blk", "rep"),
    )
    out_specs = (P("blk", None), P(("blk", "rep"), None))
    return jax.shard_map(body, mesh=mesh, in_specs=in_specs, out_specs=out_specs, check_vma=False)
```

```python
import jax
import jax.numpy as jnp
from jax import lax
from jax.experimental import pallas as pl
from jax.experimental.pallas import tpu as pltpu
from jax.sharding import PartitionSpec as P

learn_rate = 0.5
weight_decay = 0.1
TILE = 128
SLOTS = 4
XS, YS, ZS, CORES = 2, 4, 4, 2
RING = 4
PAIR = 2


def place(index):
    return (
        index // (YS * ZS * CORES),
        index // (ZS * CORES) % YS,
        index // CORES % ZS,
        index % CORES,
    )


def moved(index, way):
    at = [(a + d) % n for a, d, n in zip(place(index), way, (XS, YS, ZS, CORES))]
    return ((at[0] * YS + at[1]) * ZS + at[2]) * CORES + at[3]


def fetch(block, x=0, y=0, z=0, core=0):
    count = XS * YS * ZS * CORES
    route = [(moved(i, (x, y, z, core)), i) for i in range(count)]
    return lax.ppermute(block, "blk", route)


def exchange_along_y(blocks):
    lines = [
        [((x * YS + y) * ZS + z) * CORES + core for y in range(YS)]
        for x in range(XS)
        for z in range(ZS)
        for core in range(CORES)
    ]
    return lax.all_to_all(blocks, "blk", 0, 0, axis_index_groups=lines, tiled=True)


def adagrad(param, squares, grad, num_slabs):
    step_grad = grad / num_slabs + weight_decay * param
    total = squares + step_grad * step_grad
    return param - learn_rate * step_grad / jnp.sqrt(total)


def owner_at(here, part, step, lane):
    x, y, z, _ = here
    if part == 0:
        return (x * YS + (y + lane) % YS) * ZS + (z + step) % ZS
    return ((1 - x) * YS + (y + step) % YS) * ZS + (z + lane) % ZS


def tile_kernel(pieces, outs, last, *refs):
    size = len(pieces)
    device_ref, near_ref, far_ref, near_live, far_live, own_ratings, own_masks = refs[:7]
    far_ratings, far_masks = refs[7:9]
    item_rows = refs[9 : 9 + size]
    user_rows, user_cols, user_before = refs[9 + size : 12 + size]
    item_out = refs[12 + size : 12 + size + len(outs)]
    after = 12 + size + len(outs)
    if last:
        user_near, user_far = refs[after : after + 2]
        user_grad = refs[-1]
    else:
        user_grad = refs[after]
    after += 1 + last
    owners_ref, rows_ref, grads_ref, ratings, masks, tile_sems, row_sems, out_sems = refs[
        after : after + 8
    ]
    here = place(device_ref[0])
    core = here[3]
    blocks = user_rows.shape[0] // 2
    total = rows_ref.shape[0]

    def tile_copies(n):
        owner = owners_ref[n]
        near, far = pl.ds(0, SLOTS), pl.ds(SLOTS, SLOTS)
        pairs = (
            (own_ratings.at[owner, core], ratings.at[n, near]),
            (own_masks.at[owner, core], masks.at[n, near]),
            (far_ratings.at[owner, core], ratings.at[n, far]),
            (far_masks.at[owner, core], masks.at[n, far]),
        )
        return [
            pltpu.make_async_copy(source, target, tile_sems.at[n, i])
            for i, (source, target) in enumerate(pairs)
        ]

    row_copies, at = [], 0
    if user_before is not None:
        row_copies.append(pltpu.make_async_copy(user_before, user_grad, row_sems.at[total]))
        row_copies[-1].start()
    for a, (part, step, first, lanes) in enumerate(pieces):
        for lane in range(lanes):
            source = (here[1] + lane) % YS if part == 0 else lane
            row_copies.append(
                pltpu.make_async_copy(
                    item_rows[a].at[source], rows_ref.at[at + lane], row_sems.at[at + lane]
                )
            )
            row_copies[-1].start()
        for lane in range(lanes):
            owners_ref[at + lane] = owner_at(here, part, step, first + lane)
            for copy in tile_copies(at + lane):
                copy.start()
        at += lanes
    out_copies = [
        pltpu.make_async_copy(grads_ref.at[pl.ds(b * RING, RING)], item_out[b], out_sems.at[b])
        for b in range(len(outs))
    ]
    if user_before is None:
        user_grad[...] = jnp.zeros_like(user_grad)
    for copy in row_copies:
        copy.wait()

    def predict(n, live, tiles):
        rows = rows_ref[n]
        first = (owners_ref[n] * CORES + core) * SLOTS
        places = []
        for t in range(tiles):
            far = t >= live[0]
            slot = jnp.where(far, jnp.minimum(t - live[0], SLOTS - 1), t)
            at = first + slot
            code = jnp.where(far, far_ref[0, at] + 2 * blocks, near_ref[0, at])
            block, within = code // 2, code % 2
            alive = t < live[0] + live[1]
            places.append((jnp.where(far, slot + SLOTS, slot), block, within, alive))
        picked = jnp.concatenate([user_rows[block] for _, block, _, _ in places], 0)
        predicted = lax.dot_general(
            picked, rows, (((1,), (1,)), ((), ())), preferred_element_type=jnp.float32
        )
        return places, rows, predicted

    def residuals(n, places, predicted):
        wide = []
        for t, (slot, _, within, alive) in enumerate(places):
            part = predicted[t * TILE : (t + 1) * TILE]
            second = within == 1
            chosen = jnp.where(second, part[:, TILE:], part[:, :TILE])
            observed = jnp.maximum(masks[n, slot].astype(jnp.float32), 0.0)
            residual = observed * (chosen - ratings[n, slot].astype(jnp.float32))
            residual = residual.astype(jnp.bfloat16)
            none = jnp.zeros_like(residual)
            low = jnp.where(jnp.logical_and(alive, within == 0), residual, none)
            high = jnp.where(jnp.logical_and(alive, second), residual, none)
            wide.append(jnp.concatenate([low, high], 1))
        return jnp.concatenate(wide, 0)

    def together(entries, lives, tiles):
        firsts = [predict(n, live, tiles) for n, live in zip(entries, lives)]
        wides = [
            residuals(n, places, predicted)
            for n, (places, _, predicted) in zip(entries, firsts)
        ]
        user_parts = []
        for n, (places, rows, _), wide in zip(entries, firsts, wides):
            user_parts.append(jnp.dot(wide, rows, preferred_element_type=jnp.float32))
            turned = jnp.concatenate([user_cols[block] for _, block, _, _ in places], 1)
            grads_ref[n] = jnp.dot(turned, wide, preferred_element_type=jnp.float32).astype(
                jnp.bfloat16
            )
        for (places, _, _), user_part in zip(firsts, user_parts):
            for t, (_, block, _, _) in enumerate(places):
                user_grad[block] += user_part[t * TILE : (t + 1) * TILE]

    def some(i, carry):
        entries = [i * PAIR + k for k in range(PAIR)]
        lives = []
        for n in entries:
            for copy in tile_copies(n):
                copy.wait()
            at = owners_ref[n] * CORES + core
            lives.append((near_live[0, at], far_live[0, at]))
        most = jnp.maximum(*[live[0] + live[1] for live in lives])
        for tiles in range(2, 2 * SLOTS + 1):
            pl.when(most == tiles)(lambda tiles=tiles: together(entries, lives, tiles))
        for b, copy in enumerate(out_copies):
            pl.when(i == (b + 1) * (RING // PAIR) - 1)(copy.start)
        return carry

    lax.fori_loop(0, total // PAIR, some, 0)
    if last:
        user_near[...] = user_grad[pl.ds(0, blocks)]
        user_far[...] = user_grad[pl.ds(blocks, blocks)].astype(user_far.dtype)
    for copy in out_copies:
        copy.wait()


def tile_terms(pieces, outs, device, indices, own_tiles, far_tiles, item_rows, user_rows, user_cols, user_before, last):
    _, rows, columns = item_rows[0].shape
    blocks = user_rows.shape[0]
    total = sum(piece[3] for piece in pieces)
    smem = pl.BlockSpec(memory_space=pltpu.SMEM)
    vmem = pl.BlockSpec(memory_space=pltpu.VMEM)
    hbm = pl.BlockSpec(memory_space=pltpu.HBM)
    anywhere = pl.BlockSpec(memory_space=pl.ANY)

    first = user_before is None
    users = [jax.ShapeDtypeStruct((blocks, TILE, columns), jnp.float32)]
    if last:
        half = (blocks // 2, TILE, columns)
        users = [jax.ShapeDtypeStruct(half, jnp.float32), jax.ShapeDtypeStruct(half, jnp.bfloat16)]

    def kernel(*refs):
        cut = 11 + len(pieces)
        tile_kernel(pieces, outs, last, *refs[:cut], *((None,) if first else ()), *refs[cut:])

    result = pl.pallas_call(
        kernel,
        out_shape=[jax.ShapeDtypeStruct((RING, columns, rows), jnp.bfloat16)] * len(outs)
        + users,
        in_specs=[smem] * 5 + [hbm] * 4 + [anywhere] * len(pieces) + [vmem] * 2
        + [anywhere] * (not first),
        out_specs=[anywhere] * len(outs) + [vmem] * len(users),
        scratch_shapes=[
            pltpu.SMEM((total,), jnp.int32),
            pltpu.VMEM((total, rows, columns), jnp.bfloat16),
            pltpu.VMEM((total, columns, rows), jnp.bfloat16),
            pltpu.VMEM((total, 2 * SLOTS, TILE, TILE), jnp.bfloat16),
            pltpu.VMEM((total, 2 * SLOTS, TILE, TILE), jnp.bfloat16),
            pltpu.SemaphoreType.DMA((total, 4)),
            pltpu.SemaphoreType.DMA((total + 1,)),
            pltpu.SemaphoreType.DMA((len(outs),)),
        ]
        + [pltpu.VMEM((blocks, TILE, columns), jnp.float32)] * last,
        compiler_params=pltpu.CompilerParams(vmem_limit_bytes=(total + 12) << 20),
        cost_estimate=pl.CostEstimate(
            flops=total * (3 << 28), bytes_accessed=total << 20, transcendentals=0
        ),
    )(device, *indices, *own_tiles, *far_tiles, *item_rows, user_rows, user_cols, *(() if first else (user_before,)))
    return result[: len(outs)], result[len(outs) :]


def in_hbm(array):
    return pltpu.with_memory_space_constraint(array, pltpu.HBM)


def added(*terms):
    return sum(term.astype(jnp.float32) for term in terms)


def body(
    user_factors,
    item_factors,
    user_accum,
    item_accum,
    ratings,
    masks,
    tile_users,
    tile_items,
    tile_counts,
):
    low = jnp.bfloat16
    num_slabs = lax.axis_size("blk")
    columns = user_factors.shape[1]
    owners = num_slabs // CORES
    device = lax.axis_index("blk")

    near = tile_users * 2 + tile_items % 2
    far, far_live = fetch(near, core=1), fetch(tile_counts, core=1)
    item_low = item_factors.astype(low)
    cross = fetch(item_low, x=1)
    item_low, user_given = lax.optimization_barrier((item_low, user_factors))
    user_low = user_given.astype(low).reshape(-1, TILE, columns)
    blocks = user_low.shape[0]
    far_rows = fetch(user_low, core=1)
    shape = (owners, CORES, SLOTS, TILE, TILE)
    own_tiles = [ratings.reshape(shape), masks.reshape(shape)]
    first, second, cross, far, far_live, far_rows = lax.optimization_barrier(
        (*own_tiles, cross, far, far_live, far_rows)
    )
    far_tiles = [fetch(first, core=1), fetch(second, core=1)]
    user_rows = jnp.concatenate([user_low, far_rows], 0)

    own_line = exchange_along_y(jnp.broadcast_to(item_low, (YS,) + item_low.shape))
    far_line = [cross] + [fetch(cross, z=d) for d in range(1, RING)]
    own_line, far_line[1], far_line[2] = lax.optimization_barrier((own_line, far_line[1], far_line[2]))
    user_cols = user_rows.swapaxes(1, 2)
    rows = [own_line, jnp.stack(far_line)]
    ahead = [fetch(rows[0], z=1), fetch(rows[1], y=1)]
    behind = [fetch(rows[0], z=-1), fetch(rows[1], y=-1)]

    def terms(pieces, outs, item_rows, user_before, last=False):
        return tile_terms(
            pieces,
            outs,
            device[None],
            (near, far, tile_counts, far_live),
            [in_hbm(array) for array in own_tiles],
            [in_hbm(array) for array in far_tiles],
            item_rows,
            user_rows,
            user_cols,
            user_before,
            last,
        )

    here_terms, (user_first,) = terms(
        ((0, 0, 0, RING), (1, 0, 0, RING)), ((0, 0), (1, 0)), rows, None
    )
    rows, ahead, behind, here_terms, user_first = lax.optimization_barrier(
        (rows, ahead, behind, here_terms, user_first)
    )
    across = [fetch(rows[0], z=2), fetch(rows[1], y=2)]
    near_terms, (user_second,) = terms(
        ((0, 1, 0, RING), (1, 1, 0, RING), (0, 3, 0, RING), (1, 3, 0, RING)),
        ((0, 1), (1, 1), (0, 3), (1, 3)),
        [ahead[0], ahead[1], behind[0], behind[1]],
        user_first,
    )
    across_terms, (user_near, user_far) = terms(
        ((0, 2, 0, RING), (1, 2, 0, RING)), ((0, 2), (1, 2)), across, user_second, True
    )
    arrived = [
        [fetch(near_terms[0], z=-1), fetch(near_terms[2], z=1)],
        [fetch(near_terms[1], y=-1), fetch(near_terms[3], y=1)],
    ]
    far_grad = fetch(user_far, core=1)
    arrived, across_terms, far_grad = lax.optimization_barrier((arrived, across_terms, far_grad))
    half = (user_near + far_grad.astype(jnp.float32)).astype(low)
    arrived[0].append(fetch(across_terms[0], z=2))
    arrived[1].append(fetch(across_terms[1], y=2))
    other = lax.ppermute(half, "rep", [(0, 1), (1, 0)])

    def lines(part):
        return [
            added(here_terms[part][k], *[a[k] for a in arrived[part]]).astype(low)
            for k in range(RING)
        ]

    far_sum, own_sum = lines(1), lines(0)
    cross_sum = added(far_sum[0], *[fetch(far_sum[d], z=-d) for d in range(1, RING)]).astype(low)
    own_sum, other = lax.optimization_barrier((own_sum, other))
    user_sum = added(half, other)
    item_sum = added(
        own_sum[0],
        *[fetch(own_sum[d], y=-d) for d in range(1, RING)],
        fetch(cross_sum, x=1),
    ).T
    new_users = adagrad(user_factors, user_accum, user_sum.reshape(user_factors.shape), num_slabs)
    new_items = adagrad(item_factors, item_accum, item_sum, num_slabs)
    return (new_users, new_items)


def solution(mesh):
    in_specs = (
        P("blk", None),
        P(("blk", "rep"), None),
        P("blk", None),
        P(("blk", "rep"), None),
        P("blk", "rep", None, None),
        P("blk", "rep", None, None),
        P("blk", "rep"),
        P("blk", "rep"),
        P("blk", "rep"),
    )
    out_specs = (P("blk", None), P(("blk", "rep"), None))
    return jax.shard_map(body, mesh=mesh, in_specs=in_specs, out_specs=out_specs, check_vma=False)
```
